256 devices in a mesh: row: 16 (over z_hi, y), col: 4 (over z_lo, core), depth: 4 (over x).
Axes of the slice: x: 4, y: 4, z: 8 (z_hi: 4, z_lo: 2; z = z_hi * 2 + z_lo), core: 2. Of those that a mesh axis runs over, the one named last changes fastest.
Arguments:
- integrals: float32 [32768, 4096], P(('row', 'col'), 'depth'), may hold values from -0.09375 to 0.09375
- amplitudes: float32 [4096, 64, 64], P('depth', 'col', 'row'), may hold values from -6 to 6
Outputs:
- relaid: float32 [64, 64, 32768], P(('col', 'depth'), 'row')
The draws below stay inside these ranges and needn't reach their ends.
All inputs are finite; a program needn't handle non-finite values.
Results may differ from the reference program's by a relative error of at most 0.00007.
Values sent between devices are 32-bit elements; how exact they have to be, the bound alone decides.
No kernel may reach another device: no remote copies, remote signals or barrier semaphores. Data moves between devices by JAX's collectives and lax.ppermute only.
A program may use at most 64 MiB of HBM per device.

```python
import jax
import jax.numpy as jnp
from jax import lax

O = 64
AB = 32768
KC = 4096
N_ROW = 16


def levels(stream_key, extent, split, low, largest):
    factor_of, own = 1.0, jax.random.fold_in(stream_key, 6)
    for position, parts in split:
        draws = jnp.exp(jax.random.uniform(jax.random.fold_in(own, position), (parts,), jnp.float32, low / len(split), largest / len(split)))
        factor_of = factor_of * jnp.repeat(draws, extent[position] // parts).reshape([-1 if axis == position else 1 for axis in range(len(extent))])
    return factor_of


def gaussian(stream_key, dims, scale, reach, split=(), dtype=jnp.bfloat16):
    drawn = jax.random.normal(stream_key, dims, jnp.float32) * scale
    if len(split) > 0:
        drawn = levels(stream_key, dims, split, -0.22, 0.18) * drawn
    return jnp.clip(drawn, min=-reach, max=reach).astype(dtype)


def setup_inputs(seed: int = 0) -> dict:
    arg_keys = jax.random.split(jax.random.key(seed), 3)
    integrals = gaussian(arg_keys[0], (AB, KC), KC ** -0.5, 0.09375, ((0, 64), (1, 4)), jnp.float32)
    amplitudes = gaussian(arg_keys[1], (KC, O, O), 1.0, 6.0, ((0, 4), (1, 4), (2, 16)), jnp.float32)
    return dict(integrals=integrals, amplitudes=amplitudes)


def reference(integrals, amplitudes):
    shaped = amplitudes.reshape(KC, O, O // N_ROW, N_ROW)
    relaid = jnp.einsum("ak,kitr->irta", integrals, shaped, precision=lax.Precision.HIGHEST, preferred_element_type=jnp.float32)
    return relaid.reshape(O, O, AB)
```

```python
import functools

import jax
import jax.numpy as jnp
import numpy as np
from jax import lax
from jax.experimental import pallas as pl
from jax.experimental.pallas import tpu as pltpu
from jax.sharding import Mesh
from jax.sharding import PartitionSpec as P

AXES = ("zh", "y", "zl", "c", "x")
SIZES = (4, 4, 2, 2, 4)
VMEM = 48 * 2**20
F32, BF16 = jnp.float32, jnp.bfloat16


def move(value, y=0, z=0, c=0):
    pairs = []
    for source, (at_zh, at_y, at_zl, at_c, at_x) in enumerate(np.ndindex(*SIZES)):
        to_z = (2 * at_zh + at_zl + z) % 8
        to = (to_z // 2, (at_y + y) % 4, to_z % 2, (at_c + c) % 2, at_x)
        pairs.append((source, int(np.ravel_multi_index(to, SIZES))))
    return lax.ppermute(value, AXES, pairs)


def split(value):
    high = value.astype(BF16)
    return high, (value - high.astype(F32)).astype(BF16)


def product(t_high, t_low, w):
    w_high, w_low = split(w)
    dot = functools.partial(lax.dot_general, dimension_numbers=(((1,), (1,)), ((), ())), preferred_element_type=F32)
    return dot(t_high, w_high) + (dot(t_high, w_low) + dot(t_low, w_high))


def first_kernel(place, s0, s1, s2, s3, w0, w1, out, t_high, t_low, t):
    step = pl.program_id(0)

    @pl.when(step == 0)
    def _():
        for d, shard in enumerate((s0, s1, s2, s3)):
            at = lax.rem(place[0] + d, 4)
            for x in range(4):
                for j in range(4):
                    t[x, at, 4 * j : 4 * j + 4, :] = shard[4 * x : 4 * x + 4, j, :]
        high, low = split(t[...].reshape(256, -1))
        t_high[...] = high
        t_low[...] = low

    def work(w):
        out[...] = product(t_high[...], t_low[...], w[...]).reshape(out.shape)

    pl.when(step < 2)(lambda: work(w0))
    pl.when(step >= 2)(lambda: work(w1))


def first(place, parts, w0, w1):
    kc = w0.shape[1]
    whole = pl.BlockSpec((16, 4, kc), lambda s: (0, 0, 0))
    return pl.pallas_call(
        first_kernel,
        grid=(4,),
        in_specs=[
            pl.BlockSpec(memory_space=pltpu.SMEM),
            *[whole] * 4,
            pl.BlockSpec((256, kc), lambda s: (jnp.minimum(s, 1), 0)),
            pl.BlockSpec((256, kc), lambda s: (jnp.maximum(s - 2, 0), 0)),
        ],
        out_specs=[
            pl.BlockSpec((4, 64, 256), lambda s: (0, 0, s)),
            pl.BlockSpec((256, kc), lambda s: (0, 0)),
            pl.BlockSpec((256, kc), lambda s: (0, 0)),
        ],
        out_shape=[
            jax.ShapeDtypeStruct((4, 64, 1024), F32),
            jax.ShapeDtypeStruct((256, kc), BF16),
            jax.ShapeDtypeStruct((256, kc), BF16),
        ],
        scratch_shapes=[pltpu.VMEM((4, 4, 16, kc), F32)],
        compiler_params=pltpu.CompilerParams(vmem_limit_bytes=VMEM),
        cost_estimate=pl.CostEstimate(flops=6 * 256 * 1024 * kc, bytes_accessed=10 * 2**20, transcendentals=0),
    )(place, *parts, w0, w1)


def second_kernel(*refs):
    groups, (w0, w1, out) = refs[:8], refs[8:]

    def work(w):
        for d in range(4):
            block = product(groups[2 * d][...], groups[2 * d + 1][...], w[...])
            out[:, :, 4 * d : 4 * d + 4, :] = block.reshape(4, 16, 4, -1)

    step = pl.program_id(0)
    pl.when(step < 1)(lambda: work(w0))
    pl.when(step >= 1)(lambda: work(w1))


def second(groups, w0, w1):
    kc = w0.shape[1]
    pair = pl.BlockSpec((256, kc), lambda s: (0, 0))
    return pl.pallas_call(
        second_kernel,
        grid=(2,),
        in_specs=[pair] * 10,
        out_specs=pl.BlockSpec((4, 16, 16, 256), lambda s: (0, 0, 0, s)),
        out_shape=jax.ShapeDtypeStruct((4, 16, 16, 512), F32),
        compiler_params=pltpu.CompilerParams(vmem_limit_bytes=VMEM),
        cost_estimate=pl.CostEstimate(flops=6 * 1024 * 512 * kc, bytes_accessed=9 * 2**20, transcendentals=0),
    )(*[g for pair in groups for g in pair], w0, w1)


def place_kernel(place, part, *rest):
    out = rest[-1]
    at = pl.program_id(0) // 4
    for d in range(4):
        t = lax.rem(at + d, 4)
        for i in range(4):
            out[i, pl.ds(t, 1), :] = part[0, 4 * d + i : 4 * d + i + 1, :]


def placed(place, part, width, column, out=None):
    n = part.shape[2] // width
    return pl.pallas_call(
        place_kernel,
        grid_spec=pltpu.PrefetchScalarGridSpec(
            num_scalar_prefetch=1,
            grid=(16, n),
            in_specs=[pl.BlockSpec((1, 16, width), lambda s, q, p: (s, 0, q))]
            + ([] if out is None else [pl.BlockSpec(memory_space=pl.ANY)]),
            out_specs=pl.BlockSpec((4, 4, width), lambda s, q, p: (0, 0, column(s, q, p))),
        ),
        out_shape=jax.ShapeDtypeStruct((4, 4, 32768), F32),
        input_output_aliases={} if out is None else {2: 0},
        compiler_params=pltpu.CompilerParams(vmem_limit_bytes=VMEM),
        cost_estimate=pl.CostEstimate(flops=0, bytes_accessed=8 * part.size, transcendentals=0),
    )(place, part, *([] if out is None else [out]))


def own_column(s, q, p):
    return s * 4 + p[1] * 2 + lax.rem(p[2] + q, 2)


def next_column(step, half):
    def column(s, q, p):
        z = lax.rem(2 * (s // 4) + p[1] + step + 8, 8)
        return 2 * (((z // 2) * 4 + lax.rem(s, 4)) * 4 + lax.rem(z, 2) * 2 + lax.rem(p[2] + q, 2)) + half

    return column


def shards(integrals, amplitudes):
    place = jnp.stack([lax.axis_index(n).astype(jnp.int32) for n in ("y", "zl", "c")])
    t0 = jnp.transpose(amplitudes, (1, 2, 0))

    def along_y(t):
        return t, move(t, y=-1), move(t, y=2), move(t, y=1)

    w1 = move(integrals, c=1)
    near = [along_y(t0)]
    t1, t3 = move(t0, z=-2), move(t0, z=2)
    t2 = move(t0, z=4)
    up, down = move(integrals[256:], z=1), move(integrals[:256], z=-1)
    up1, down1 = move(up, c=1), move(down, c=1)
    near += [along_y(t) for t in (t1, t2, t3)]

    def summed(part):
        return lax.psum_scatter(part, "x", scatter_dimension=0)

    sums, groups = [], [None] * 4
    for d in (0, 1, 3, 2):
        part, *groups[d] = first(place, near[d], integrals, w1)
        sums.append((d, summed(part)))
    sums = [s.reshape(16, 4, 1024) for _, s in sorted(sums, key=lambda pair: pair[0])]

    def relaid(value):
        return lax.all_to_all(value, ("zh", "y"), split_axis=0, concat_axis=0, tiled=True)

    own = relaid(jnp.concatenate(sums, axis=1))
    third = relaid(summed(second(groups, down, down1)))
    fourth = relaid(summed(second(groups, up, up1)))
    out = placed(place, own, 512, own_column)
    out = placed(place, third, 256, next_column(1, 0), out)
    return placed(place, fourth, 256, next_column(-1, 1), out)


def solution(mesh):
    fine = Mesh(mesh.devices.reshape(SIZES), AXES)
    return jax.shard_map(
        shards,
        mesh=fine,
        in_specs=(P(("zh", "y", "zl", "c"), "x"), P("x", ("zl", "c"), ("zh", "y"))),
        out_specs=P(("zl", "c", "x"), ("zh", "y"), None),
        check_vma=False,
    )
```

```python
import functools

import jax
import jax.numpy as jnp
import numpy as np
from jax import lax
from jax.experimental import pallas as pl
from jax.experimental.pallas import tpu as pltpu
from jax.sharding import Mesh
from jax.sharding import PartitionSpec as P

AXES = ("zh", "y", "zl", "c", "x")
SIZES = (4, 4, 2, 2, 4)
VMEM = pl.BlockSpec(memory_space=pltpu.VMEM)
SMEM = pl.BlockSpec(memory_space=pltpu.SMEM)
HBM = pl.BlockSpec(memory_space=pltpu.MemorySpace.HBM)
F32, BF16 = jnp.float32, jnp.bfloat16


def move(value, x=0, y=0, z=0, c=0, apart=0):
    pairs = []
    for source, (at_zh, at_y, at_zl, at_c, at_x) in enumerate(np.ndindex(*SIZES)):
        to_z = (2 * at_zh + at_zl + z + (2 * at_c - 1) * apart) % 8
        to = (to_z // 2, (at_y + y) % 4, to_z % 2, (at_c + c) % 2, (at_x + x) % 4)
        pairs.append((source, int(np.ravel_multi_index(to, SIZES))))
    return lax.ppermute(value, AXES, pairs)


def after(value, *others):
    return lax.optimization_barrier((value, others))[0]


def call(kernel, args, shapes, scratch=(), place=None, in_hbm=(), out_hbm=(), aliases=None, limit=12):
    count = len(args)
    specs = [HBM if n in in_hbm else VMEM for n in range(count)]
    if place is not None:
        args, specs = [place, *args], [SMEM, *specs]
    return pl.pallas_call(
        kernel,
        in_specs=specs,
        out_specs=[HBM if n in out_hbm else VMEM for n in range(len(shapes))],
        out_shape=[jax.ShapeDtypeStruct(*shape) for shape in shapes],
        scratch_shapes=list(scratch),
        input_output_aliases=aliases or {},
        compiler_params=pltpu.CompilerParams(vmem_limit_bytes=limit * 2**20),
        cost_estimate=pl.CostEstimate(flops=0, bytes_accessed=0, transcendentals=0),
    )(*args)


def split(value):
    high = value.astype(BF16)
    return high, (value - high.astype(F32)).astype(BF16)


def turn_kernel(place, value, out):
    for j in range(4):
        out[j] = value[:, j, :]


def halved_kernel(value, high, low):
    high[...], low[...] = split(value[...])


def halved(value):
    return call(halved_kernel, [value], [(value.shape, BF16)] * 2)


def pair_kernel(one, other, out):
    out[0] = one[...]
    out[1] = other[...]


def pair(one, other):
    return call(pair_kernel, [one, other], [((2, *one.shape), F32)])[0]


def forward_kernel(own, low, high, to_right, to_left):
    for out, come, start in ((to_right, low, 0), (to_left, high, 8)):
        out[:, :16] = own[...]
        out[:, 16:24] = come[0, :, start : start + 8]
        out[:, 24:] = come[1, :, start : start + 8]


def forward(own, low, high):
    shape = (4, 32, own.shape[2])
    to_right, to_left = call(forward_kernel, [own, low, high], [(shape, F32)] * 2)
    return move(to_right, y=1), move(to_left, y=-1)


def product(t_high, t_low, w_high, w_low):
    dot = functools.partial(lax.dot_general, dimension_numbers=(((1,), (1,)), ((), ())), preferred_element_type=F32)
    return dot(t_high, w_high) + (dot(t_high, w_low) + dot(t_low, w_high))


def store(blocks, at, outs):
    half = blocks.shape[1] // 2
    columns = slice(at, at + blocks.shape[2])
    to_right, to_left, right_low, left_high, own = outs
    to_right[:half, columns] = blocks[2, :half]
    to_right[half:, columns] = blocks[1, half:]
    to_left[:half, columns] = blocks[2, half:]
    to_left[half:, columns] = blocks[3, :half]
    right_low[:, columns] = blocks[1, :half]
    left_high[:, columns] = blocks[3, half:]
    own[:, columns] = blocks[0]


def shapes_of(rows, columns):
    return [((n, columns), F32) for n in (rows, rows, rows // 2, rows // 2, rows)]


def first_kernel(sources, n_parts, place, *refs):
    n = len(sources)
    parts, ws, outs = refs[:n_parts], refs[n_parts : n_parts + 4], refs[n_parts + 4 : n_parts + 9]
    split_t, t = refs[n_parts + 9 : -1], refs[-1]
    for g, group in enumerate(sources):
        for d, halves in enumerate(group):
            at = lax.rem(place[0] + d, 4)
            for x in range(4):
                number, lead, start = halves[x // 2]
                part = parts[number] if lead is None else parts[number].at[lead]
                start = start + 4 * (x % 2)
                e = lax.rem(x - place[3] + 4, 4)
                for j in range(4):
                    t[e, at, 4 * j : 4 * j + 4, :] = part[j, start : start + 4, :]
        split_t[2 * g][...], split_t[2 * g + 1][...] = split(t[...].reshape(256, -1))
    for k in range(4):
        rows = slice(256 * (k % 2), 256 * (k % 2) + 256)
        w_high, w_low = ws[k // 2 * 2][rows, :], ws[k // 2 * 2 + 1][rows, :]
        blocks = [product(split_t[2 * g][...], split_t[2 * g + 1][...], w_high, w_low) for g in range(n)]
        blocks = [block.reshape(4, 64, 256) for block in blocks]
        store(blocks[0] if n == 1 else jnp.concatenate(blocks, axis=1), 256 * k, outs)


def first(place, sources, parts, w0, w1):
    kc, n = w0[0].shape[1], len(sources)
    out = call(
        functools.partial(first_kernel, sources, len(parts)),
        [*parts, *w0, *w1],
        shapes_of(64 * n, 1024) + [((256, kc), BF16)] * (2 * n),
        [pltpu.VMEM((4, 4, 16, kc), F32)],
        place,
        limit=16,
    )
    return out[:5], [out[5 + 2 * g : 7 + 2 * g] for g in range(n)]


def second_kernel(half, place, *refs):
    groups, w, (out, buffer, sems) = refs[:8], refs[8], refs[-3:]
    copies = []
    for n in range(2):
        w_high, w_low = split(w[256 * n : 256 * n + 256, :])
        for d in range(4):
            block = product(groups[2 * d][...], groups[2 * d + 1][...], w_high, w_low)
            buffer[n, :, :, 4 * d : 4 * d + 4, :] = block.reshape(4, 16, 4, 256)
        for e in range(4):
            to = out.at[lax.rem(place[3] + e, 4), :, :, pl.ds(512 * half + 256 * n, 256)]
            copies.append(pltpu.make_async_copy(buffer.at[n, e], to, sems.at[n, e]))
            copies[-1].start()
    for copy in copies:
        copy.wait()


def second(place, groups, w, half, out=None):
    args = [g for pair in groups for g in pair] + [w]
    return call(
        functools.partial(second_kernel, half),
        args if out is None else [*args, out],
        [((4, 16, 16, 1024), F32)],
        [pltpu.VMEM((2, 4, 16, 16, 256), F32), pltpu.SemaphoreType.DMA((2, 4))],
        place,
        in_hbm=(9,),
        out_hbm=(0,),
        aliases=None if out is None else {10: 0},
    )[0]


def add_kernel(right_low, left_high, from_left, from_right, to_right, to_left):
    half = right_low.shape[0]
    to_right[...] = right_low[...] + from_left[:half]
    to_left[...] = left_high[...] + from_right[:half]


def ring_first(parts):
    return move(parts[0], x=1), move(parts[1], x=-1)


def ring_second(parts, come):
    to_right, to_left = call(add_kernel, [*parts[2:4], *come], [(parts[2].shape, F32)] * 2)
    return [parts[4], *come, move(to_right, x=1), move(to_left, x=-1)]


def total(own, from_left, from_right, from_left2, from_right2):
    half = own.shape[0] // 2
    low = own[:half] + from_right[half:] + from_left2[...]
    high = own[half:] + from_left[half:] + from_right2[...]
    return jnp.concatenate([low, high])


def collect_kernel(*refs):
    out = refs[-1]
    sums = [total(*refs[5 * u : 5 * u + 5]) for u in range(3)]
    for d, value in enumerate([sums[0], sums[1][:64], sums[2], sums[1][64:]]):
        out[:, 4 * d : 4 * d + 4, :] = value.reshape(16, 4, -1)


def collect(sums):
    return call(collect_kernel, [term for terms in sums for term in terms], [((16, 16, 1024), F32)])[0]


def place_kernel(column, n_parts, place, *refs):
    parts, (out, block, done) = refs[:n_parts], refs[-3:]
    pieces = [(part, at) for part in parts for at in range(0, part.shape[2], 512)]
    copies = []
    for s in range(16):
        for q, (part, at) in enumerate(pieces):
            for d in range(4):
                block[q, s, :, (s // 4 + d) % 4, :] = part[s, 4 * d : 4 * d + 4, at : at + 512]
            columns = pl.ds(pl.multiple_of(512 * column(place, s, q), 512), 512)
            copies.append(pltpu.make_async_copy(block.at[q, s], out.at[:, :, columns], done.at[16 * q + s]))
            copies[-1].start()
    for copy in copies:
        copy.wait()


def placed(place, parts, column, out=None):
    n = sum(part.shape[2] // 512 for part in parts)
    return call(
        functools.partial(place_kernel, column, len(parts)),
        parts if out is None else [*parts, out],
        [((4, 4, 32768), F32)],
        [pltpu.VMEM((n, 16, 4, 4, 512), F32), pltpu.SemaphoreType.DMA((16 * n,))],
        place,
        in_hbm=(len(parts),),
        out_hbm=(0,),
        aliases=None if out is None else {1 + len(parts): 0},
    )[0]


def own_column(place, s, q):
    return s * 4 + place[1] * 2 + lax.rem(place[2] + q, 2)


def next_column(place, s, q):
    core = lax.rem(place[2] + q, 2)
    z = lax.rem(2 * (s // 4) + place[1] + 9 - 2 * core, 8)
    return ((z // 2) * 4 + s % 4) * 4 + lax.rem(z, 2) * 2 + core


def shards(integrals, amplitudes):
    place = jnp.stack([lax.axis_index(n).astype(jnp.int32) for n in ("y", "zl", "c", "x")])
    kc = integrals.shape[1]
    (t0,) = call(turn_kernel, [jnp.transpose(amplitudes, (1, 2, 0))], [((4, 16, kc), F32)], place=place)

    t1, t3 = move(t0, z=-2), move(t0, z=2)
    low0, high0, far0 = move(t0, y=1), move(t0, y=-1), move(t0, y=2)
    w = halved(integrals)

    t1, t3, low0, high0, far0 = after((t1, t3, low0, high0, far0))
    w1 = move(after(integrals, t1), c=1)
    t13 = pair(t1, t3)
    low13, high13 = move(t13, y=1), move(t13, y=-1)
    t2 = move(after(t0, t1), z=4)
    w1 = halved(w1)

    def whole(n, lead=None):
        return ((n, lead, 0), (n, lead, 8))

    def halves(at):
        return ((2, None, at), (3, None, at))

    parts0, (group0,) = first(place, [[whole(n) for n in range(4)]], [t0, high0, far0, low0], w, w1)
    come0 = ring_first(parts0)

    t2, low13, high13 = after((t2, low13, high13), parts0, come0)
    w2 = move(after(integrals, t2), apart=1)
    low2, high2 = forward(t2, low13, high13)
    far2 = move(t2, y=2)
    sum0 = ring_second(parts0, come0)
    low2, high2, far2 = after((low2, high2, far2))
    sources = [[whole(0, g), whole(1, g), halves(16 + 8 * g), whole(4, g)] for g in range(2)]
    parts1, (group1, group3) = first(place, sources, [t13, high13, low2, high2, low13], w, w1)
    come1 = ring_first(parts1)
    parts2, (group2,) = first(place, [[whole(n) for n in range(4)]], [after(t2, parts1), high2, far2, low2], w, w1)
    come2 = ring_first(parts2)
    w3 = move(after(w2, parts1), c=1)

    groups = [group0, group1, group2, group3]
    both = second(place, groups, after(w2, sum0), 0)
    both = second(place, groups, after(w3, both, come1), 1, both)
    rest = lax.psum_scatter(both, "x", scatter_dimension=0)
    sum1 = ring_second(after(parts1, both), come1)
    sum2 = ring_second(after(parts2, both), come2)

    def relaid(value):
        return lax.all_to_all(value, ("zh", "y"), split_axis=0, concat_axis=0, tiled=True)

    out = placed(place, [relaid(collect([sum0, sum1, sum2]))], own_column)
    return placed(place, [relaid(rest)], next_column, out)


def solution(mesh):
    fine = Mesh(mesh.devices.reshape(SIZES), AXES)
    return jax.shard_map(
        shards,
        mesh=fine,
        in_specs=(P(("zh", "y", "zl", "c"), "x"), P("x", ("zl", "c"), ("zh", "y"))),
        out_specs=P(("zl", "c", "x"), ("zh", "y"), None),
        check_vma=False,
    )
```

```python
import functools

import jax
import jax.numpy as jnp
import numpy as np
from jax import lax
from jax.experimental import pallas as pl
from jax.experimental.pallas import tpu as pltpu
from jax.sharding import Mesh
from jax.sharding import PartitionSpec as P

AXES = ("zh", "y", "zl", "c", "x")
SIZES = (4, 4, 2, 2, 4)
VMEM = pl.BlockSpec(memory_space=pltpu.VMEM)
SMEM = pl.BlockSpec(memory_space=pltpu.SMEM)
HBM = pl.BlockSpec(memory_space=pltpu.MemorySpace.HBM)
F32, BF16 = jnp.float32, jnp.bfloat16


def move(value, x=0, y=0, z=0, c=0, apart=0):
    pairs = []
    for source, (at_zh, at_y, at_zl, at_c, at_x) in enumerate(np.ndindex(*SIZES)):
        to_z = (2 * at_zh + at_zl + z + (2 * at_c - 1) * apart) % 8
        to = (to_z // 2, (at_y + y) % 4, to_z % 2, (at_c + c) % 2, (at_x + x) % 4)
        pairs.append((source, int(np.ravel_multi_index(to, SIZES))))
    return lax.ppermute(value, AXES, pairs)


def after(value, *others):
    return lax.optimization_barrier((value, others))[0]


def call(kernel, args, shapes, scratch=(), place=None, in_hbm=(), out_hbm=(), aliases=None, limit=12):
    count = len(args)
    specs = [HBM if n in in_hbm else VMEM for n in range(count)]
    if place is not None:
        args, specs = [place, *args], [SMEM, *specs]
    return pl.pallas_call(
        kernel,
        in_specs=specs,
        out_specs=[HBM if n in out_hbm else VMEM for n in range(len(shapes))],
        out_shape=[jax.ShapeDtypeStruct(*shape) for shape in shapes],
        scratch_shapes=list(scratch),
        input_output_aliases=aliases or {},
        compiler_params=pltpu.CompilerParams(vmem_limit_bytes=limit * 2**20),
        cost_estimate=pl.CostEstimate(flops=0, bytes_accessed=0, transcendentals=0),
    )(*args)


def split(value):
    high = value.astype(BF16)
    return high, (value - high.astype(F32)).astype(BF16)


def turn_kernel(place, value, out):
    for j in range(4):
        out[j] = value[:, j, :]


def halved_kernel(value, high, low):
    high[...], low[...] = split(value[...])


def halved(value):
    return call(halved_kernel, [value], [(value.shape, BF16)] * 2)


def pair_kernel(one, other, out):
    out[0] = one[...]
    out[1] = other[...]


def pair(one, other):
    return call(pair_kernel, [one, other], [((2, *one.shape), F32)])[0]


def forward_kernel(own, low, high, to_right, to_left):
    for out, come, start in ((to_right, low, 0), (to_left, high, 8)):
        out[:, :16] = own[...]
        out[:, 16:24] = come[0, :, start : start + 8]
        out[:, 24:] = come[1, :, start : start + 8]


def forward(own, low, high):
    shape = (4, 32, own.shape[2])
    to_right, to_left = call(forward_kernel, [own, low, high], [(shape, F32)] * 2)
    return move(to_right, y=1), move(to_left, y=-1)


def last_kernel(low, high, to_right, to_left):
    to_right[...] = low[:, :8]
    to_left[...] = high[:, 8:16]


def last(low, high):
    shape = (4, 8, low.shape[2])
    to_right, to_left = call(last_kernel, [low, high], [(shape, F32)] * 2)
    return move(to_right, y=1), move(to_left, y=-1)


def product(t_high, t_low, w_high, w_low):
    dot = functools.partial(lax.dot_general, dimension_numbers=(((1,), (1,)), ((), ())), preferred_element_type=F32)
    return dot(t_high, w_high) + (dot(t_high, w_low) + dot(t_low, w_high))


def store(blocks, at, outs):
    half = blocks.shape[1] // 2
    columns = slice(at, at + blocks.shape[2])
    to_right, to_left, right_low, left_high, own = outs
    to_right[:half, columns] = blocks[2, :half]
    to_right[half:, columns] = blocks[1, half:]
    to_left[:half, columns] = blocks[2, half:]
    to_left[half:, columns] = blocks[3, :half]
    right_low[:, columns] = blocks[1, :half]
    left_high[:, columns] = blocks[3, half:]
    own[:, columns] = blocks[0]


def shapes_of(rows, columns):
    return [((n, columns), F32) for n in (rows, rows, rows // 2, rows // 2, rows)]


def first_kernel(sources, n_parts, place, *refs):
    n = len(sources)
    parts, ws, outs = refs[:n_parts], refs[n_parts : n_parts + 4], refs[n_parts + 4 : n_parts + 9]
    t_high, t_low, t = refs[-3:]
    for m, halves in enumerate(sources):
        for x in range(4):
            number, lead, start = halves[x // 2]
            part = parts[number] if lead is None else parts[number].at[lead]
            start = start + 4 * (x % 2)
            e = lax.rem(x - place[3] + 4, 4)
            for j in range(4):
                t[e, m, 4 * j : 4 * j + 4, :] = part[j, start : start + 4, :]
    t_high[...], t_low[...] = split(t[...].reshape(64 * n, -1))
    for k in range(4):
        rows = slice(256 * (k % 2), 256 * (k % 2) + 256)
        block = product(t_high[...], t_low[...], ws[k // 2 * 2][rows, :], ws[k // 2 * 2 + 1][rows, :])
        store(block.reshape(4, 16 * n, 256), 256 * k, outs)


def first(place, sources, parts, w0, w1):
    kc, n = w0[0].shape[1], len(sources)
    out = call(
        functools.partial(first_kernel, sources, len(parts)),
        [*parts, *w0, *w1],
        shapes_of(16 * n, 1024) + [((64 * n, kc), BF16)] * 2,
        [pltpu.VMEM((4, n, 16, kc), F32)],
        place,
        limit=16,
    )
    return out[:5], out[5:]


def second_rows(shards, place, units, w_high, w_low, buffer):
    for u, unit in enumerate(shards):
        block = product(units[2 * u][...], units[2 * u + 1][...], w_high, w_low)
        block = block.reshape(4, len(unit), 4, 4, 256)
        for m, (d, dy) in enumerate(unit):
            r = 4 * lax.rem(place[0] + dy, 4)
            buffer[:, pl.ds(r, 4), 4 * d : 4 * d + 4, :] = block[:, m]


def second_ring_kernel(shards, place, *refs):
    units, w, outs, buffer = refs[:4], refs[4], refs[5:10], refs[10]
    for n in range(2):
        second_rows(shards, place, units, *split(w[256 * n : 256 * n + 256, :]), buffer)
        store(buffer[...].reshape(4, 256, 256), 256 * n, outs)


def second_ring(place, shards, units, w):
    kernel = functools.partial(second_ring_kernel, shards)
    return call(kernel, [*units, w], shapes_of(256, 512), [pltpu.VMEM((4, 16, 16, 256), F32)], place)


def add_kernel(right_low, left_high, from_left, from_right, to_right, to_left):
    half = right_low.shape[0]
    to_right[...] = right_low[...] + from_left[:half]
    to_left[...] = left_high[...] + from_right[:half]


def ring_first(parts):
    return move(parts[0], x=1), move(parts[1], x=-1)


def ring_add(parts, come):
    return call(add_kernel, [*parts[2:4], *come], [(parts[2].shape, F32)] * 2)


def ring_second(parts, come, added):
    return [parts[4], *come, move(added[0], x=1), move(added[1], x=-1)]


def total(own, from_left, from_right, from_left2, from_right2):
    half = own.shape[0] // 2
    low = own[:half] + from_right[half:] + from_left2[...]
    high = own[half:] + from_left[half:] + from_right2[...]
    return jnp.concatenate([low, high])


def collect_kernel(shards, place, *refs):
    out = refs[-1]
    for u, unit in enumerate(shards):
        value = total(*refs[5 * u : 5 * u + 5]).reshape(len(unit), 4, 4, -1)
        for m, (d, dy) in enumerate(unit):
            out[pl.ds(4 * lax.rem(place[0] + dy, 4), 4), 4 * d : 4 * d + 4, :] = value[m]


def collect(place, shards, sums):
    args = [term for terms in sums for term in terms]
    return call(functools.partial(collect_kernel, shards), args, [((16, 16, 1024), F32)], place=place, limit=16)[0]


def join_kernel(*refs):
    out = refs[-1]
    out[:, :, :512] = total(*refs[:5]).reshape(16, 16, -1)
    out[:, :, 512:] = total(*refs[5:-1]).reshape(16, 16, -1)


def join(one, other):
    return call(join_kernel, [*one, *other], [((16, 16, 1024), F32)])[0]


def place_kernel(column, n_parts, place, *refs):
    parts, (out, block, done) = refs[:n_parts], refs[-3:]
    pieces = [(part, at) for part in parts for at in range(0, part.shape[2], 512)]
    copies = []
    for s in range(16):
        for q, (part, at) in enumerate(pieces):
            for d in range(4):
                block[q, s, :, (s // 4 + d) % 4, :] = part[s, 4 * d : 4 * d + 4, at : at + 512]
            columns = pl.ds(pl.multiple_of(512 * column(place, s, q), 512), 512)
            copies.append(pltpu.make_async_copy(block.at[q, s], out.at[:, :, columns], done.at[16 * q + s]))
            copies[-1].start()
    for copy in copies:
        copy.wait()


def placed(place, parts, column, out=None):
    n = sum(part.shape[2] // 512 for part in parts)
    return call(
        functools.partial(place_kernel, column, len(parts)),
        parts if out is None else [*parts, out],
        [((4, 4, 32768), F32)],
        [pltpu.VMEM((n, 16, 4, 4, 512), F32), pltpu.SemaphoreType.DMA((16 * n,))],
        place,
        in_hbm=(len(parts),),
        out_hbm=(0,),
        aliases=None if out is None else {1 + len(parts): 0},
    )[0]


def own_column(place, s, q):
    return s * 4 + place[1] * 2 + lax.rem(place[2] + q, 2)


def next_column(place, s, q):
    core = lax.rem(place[2] + q, 2)
    z = lax.rem(2 * (s // 4) + place[1] + 9 - 2 * core, 8)
    return ((z // 2) * 4 + s % 4) * 4 + lax.rem(z, 2) * 2 + core


def local(integrals, amplitudes):
    place = jnp.stack([lax.axis_index(n).astype(jnp.int32) for n in ("y", "zl", "c", "x")])
    kc = integrals.shape[1]
    (t0,) = call(turn_kernel, [jnp.transpose(amplitudes, (1, 2, 0))], [((4, 16, kc), F32)], place=place)

    t1, t3 = move(t0, z=-2), move(t0, z=2)
    low0, high0, far0 = move(t0, y=1), move(t0, y=-1), move(t0, y=2)
    w = halved(integrals)

    t1, t3, low0, high0, far0 = after((t1, t3, low0, high0, far0))
    t2 = move(after(t0, t1), z=4)
    t13 = pair(t1, t3)
    low13, high13 = move(t13, y=1), move(t13, y=-1)
    t2, low13, high13 = after((t2, low13, high13))
    w1 = halved(move(after(integrals, t2), c=1))
    low2, high2 = forward(t2, low13, high13)
    w2 = move(after(integrals, t2), apart=1)

    def whole(n, lead=None):
        return ((n, lead, 0), (n, lead, 8))

    def halves(at):
        return ((0, None, at), (1, None, at))

    shards = [
        [(0, 0), (0, 1), (0, 2), (0, 3), (1, 0), (1, 1), (1, 3), (3, 0), (3, 1), (3, 3)],
        [(1, 2), (3, 2), (2, 0), (2, 1), (2, 2), (2, 3)],
    ]
    sources = [whole(0), whole(1), whole(2), whole(3)] + [whole(n, g) for g in range(2) for n in (4, 5, 6)]
    parts0, unit0 = first(place, sources, [t0, high0, far0, low0, t13, high13, low13], w, w1)
    come0 = ring_first(parts0)

    low2, high2 = after((low2, high2), parts0)
    far2 = last(low2, high2)
    sources = [halves(16), halves(24), whole(4), whole(1), ((2, None, 0), (3, None, 0)), whole(0)]
    parts1, unit1 = first(place, sources, [low2, high2, *far2, t2], w, w1)
    come1 = ring_first(parts1)

    units = [*unit0, *unit1]
    added0 = ring_add(parts0, come0)
    sum0 = ring_second(parts0, come0, added0)
    added1 = ring_add(after(parts1, come0), come1)
    sum1 = ring_second(parts1, come1, added1)
    parts2 = second_ring(place, shards, units, after(w2, added1, added0))
    w3 = move(after(w2, parts1, come0, added0), c=1)
    come2 = ring_first(parts2)
    parts3 = second_ring(place, shards, units, after(w3, parts2, sum0))
    come3 = ring_first(parts3)
    sum2 = ring_second(parts2, come2, ring_add(parts2, come2))
    sum3 = ring_second(parts3, come3, ring_add(parts3, come3))

    def relaid(value):
        return lax.all_to_all(value, ("zh", "y"), split_axis=0, concat_axis=0, tiled=True)

    out = placed(place, [relaid(collect(place, shards, after([sum0, sum1], parts3, come2)))], own_column)
    return placed(place, [relaid(join(sum2, sum3))], next_column, out)


def solution(mesh):
    fine = Mesh(mesh.devices.reshape(SIZES), AXES)
    return jax.shard_map(
        local,
        mesh=fine,
        in_specs=(P(("zh", "y", "zl", "c"), "x"), P("x", ("zl", "c"), ("zh", "y"))),
        out_specs=P(("zl", "c", "x"), ("zh", "y"), None),
        check_vma=False,
    )
```

```python
import functools

import jax
import jax.numpy as jnp
import numpy as np
from jax import lax
from jax.experimental import pallas as pl
from jax.experimental.pallas import tpu as pltpu
from jax.sharding import Mesh
from jax.sharding import PartitionSpec as P

AXES = ("zh", "y", "zl", "c", "x")
SIZES = (4, 4, 2, 2, 4)
VMEM = pl.BlockSpec(memory_space=pltpu.VMEM)
SMEM = pl.BlockSpec(memory_space=pltpu.SMEM)
HBM = pl.BlockSpec(memory_space=pltpu.MemorySpace.HBM)
F32, BF16 = jnp.float32, jnp.bfloat16


def move(value, x=0, y=0, z=0, c=0, apart=0):
    pairs = []
    for source, (at_zh, at_y, at_zl, at_c, at_x) in enumerate(np.ndindex(*SIZES)):
        to_z = (2 * at_zh + at_zl + z + (2 * at_c - 1) * apart) % 8
        to = (to_z // 2, (at_y + y) % 4, to_z % 2, (at_c + c) % 2, (at_x + x) % 4)
        pairs.append((source, int(np.ravel_multi_index(to, SIZES))))
    return lax.ppermute(value, AXES, pairs)


def after(value, *others):
    return lax.optimization_barrier((value, others))[0]


def call(kernel, args, shapes, scratch=(), place=None, in_hbm=(), out_hbm=(), aliases=None, limit=12):
    count = len(args)
    specs = [HBM if n in in_hbm else VMEM for n in range(count)]
    if place is not None:
        args, specs = [place, *args], [SMEM, *specs]
    return pl.pallas_call(
        kernel,
        in_specs=specs,
        out_specs=[HBM if n in out_hbm else VMEM for n in range(len(shapes))],
        out_shape=[jax.ShapeDtypeStruct(*shape) for shape in shapes],
        scratch_shapes=list(scratch),
        input_output_aliases=aliases or {},
        compiler_params=pltpu.CompilerParams(vmem_limit_bytes=limit * 2**20),
        cost_estimate=pl.CostEstimate(flops=0, bytes_accessed=0, transcendentals=0),
    )(*args)


def split(value):
    high = value.astype(BF16)
    return high, (value - high.astype(F32)).astype(BF16)


def turn_kernel(place, value, out):
    for j in range(4):
        out[j] = value[:, j, :]


def halved_kernel(value, high, low):
    high[...], low[...] = split(value[...])


def halved(value):
    return call(halved_kernel, [value], [(value.shape, BF16)] * 2)


def pair_kernel(one, other, out):
    out[0] = one[...]
    out[1] = other[...]


def pair(one, other):
    return call(pair_kernel, [one, other], [((2, *one.shape), F32)])[0]


def forward_kernel(own, low, high, to_right, to_left):
    for out, come, start in ((to_right, low, 0), (to_left, high, 8)):
        out[:, :16] = own[...]
        out[:, 16:24] = come[0, :, start : start + 8]
        out[:, 24:] = come[1, :, start : start + 8]


def forward(own, low, high):
    shape = (4, 32, own.shape[2])
    to_right, to_left = call(forward_kernel, [own, low, high], [(shape, F32)] * 2)
    return move(to_right, y=1), move(to_left, y=-1)


def last_kernel(low, high, to_right, to_left):
    to_right[...] = low[:, :8]
    to_left[...] = high[:, 8:16]


def last(low, high):
    shape = (4, 8, low.shape[2])
    to_right, to_left = call(last_kernel, [low, high], [(shape, F32)] * 2)
    return move(to_right, y=1), move(to_left, y=-1)


def whole_kernel(low, high, out):
    out[:, :8] = low[...]
    out[:, 8:] = high[...]


def whole_of(low, high):
    return call(whole_kernel, [low, high], [((4, 16, low.shape[2]), F32)])[0]


def product(t_high, t_low, w_high, w_low):
    dot = functools.partial(lax.dot_general, dimension_numbers=(((1,), (1,)), ((), ())), preferred_element_type=F32)
    return dot(t_high, w_high) + (dot(t_high, w_low) + dot(t_low, w_high))


def store(blocks, at, outs):
    half = blocks.shape[1] // 2
    columns = slice(at, at + blocks.shape[2])
    to_right, to_left, right_low, left_high, own = outs
    to_right[:half, columns] = blocks[2, :half]
    to_right[half:, columns] = blocks[1, half:]
    to_left[:half, columns] = blocks[2, half:]
    to_left[half:, columns] = blocks[3, :half]
    right_low[:, columns] = blocks[1, :half]
    left_high[:, columns] = blocks[3, half:]
    own[:, columns] = blocks[0]


def shapes_of(rows, columns):
    return [((n, columns), F32) for n in (rows, rows, rows // 2, rows // 2, rows)]


def first_kernel(sources, n_parts, place, *refs):
    n = len(sources)
    parts, ws, outs = refs[:n_parts], refs[n_parts : n_parts + 4], refs[n_parts + 4 : n_parts + 9]
    t_high, t_low, t = refs[-3:]
    for m, halves in enumerate(sources):
        for x in range(4):
            number, lead, start = halves[x // 2]
            part = parts[number] if lead is None else parts[number].at[lead]
            start = start + 4 * (x % 2)
            e = lax.rem(x - place[3] + 4, 4)
            for j in range(4):
                t[e, m, 4 * j : 4 * j + 4, :] = part[j, start : start + 4, :]
    t_high[...], t_low[...] = split(t[...].reshape(64 * n, -1))
    for k in range(4):
        rows = slice(256 * (k % 2), 256 * (k % 2) + 256)
        block = product(t_high[...], t_low[...], ws[k // 2 * 2][rows, :], ws[k // 2 * 2 + 1][rows, :])
        store(block.reshape(4, 16 * n, 256), 256 * k, outs)


def first(place, sources, parts, w0, w1):
    kc, n = w0[0].shape[1], len(sources)
    out = call(
        functools.partial(first_kernel, sources, len(parts)),
        [*parts, *w0, *w1],
        shapes_of(16 * n, 1024) + [((64 * n, kc), BF16)] * 2,
        [pltpu.VMEM((4, n, 16, kc), F32)],
        place,
        limit=16,
    )
    return out[:5], out[5:]


def second_rows(shards, place, units, w_high, w_low, buffer):
    for u, unit in enumerate(shards):
        block = product(units[2 * u][...], units[2 * u + 1][...], w_high, w_low)
        block = block.reshape(4, len(unit), 4, 4, 256)
        for m, (d, dy) in enumerate(unit):
            r = 4 * lax.rem(place[0] + dy, 4)
            buffer[:, pl.ds(r, 4), 4 * d : 4 * d + 4, :] = block[:, m]


def second_ring_kernel(shards, place, *refs):
    units, w, outs, buffer = refs[:4], refs[4], refs[5:10], refs[10]
    for n in range(2):
        second_rows(shards, place, units, *split(w[256 * n : 256 * n + 256, :]), buffer)
        store(buffer[...].reshape(4, 256, 256), 256 * n, outs)


def second_ring(place, shards, units, w):
    kernel = functools.partial(second_ring_kernel, shards)
    return call(kernel, [*units, w], shapes_of(256, 512), [pltpu.VMEM((4, 16, 16, 256), F32)], place)


def add_kernel(right_low, left_high, from_left, from_right, to_right, to_left):
    half = right_low.shape[0]
    to_right[...] = right_low[...] + from_left[:half]
    to_left[...] = left_high[...] + from_right[:half]


def ring_first(parts):
    return move(parts[0], x=1), move(parts[1], x=-1)


def ring_add(parts, come):
    return call(add_kernel, [*parts[2:4], *come], [(parts[2].shape, F32)] * 2)


def ring_second(parts, come, added):
    return [parts[4], *come, move(added[0], x=1), move(added[1], x=-1)]


def total(own, from_left, from_right, from_left2, from_right2):
    half = own.shape[0] // 2
    low = own[:half] + from_right[half:] + from_left2[...]
    high = own[half:] + from_left[half:] + from_right2[...]
    return jnp.concatenate([low, high])


def collect_kernel(shards, place, *refs):
    out = refs[-1]
    for u, unit in enumerate(shards):
        value = total(*refs[5 * u : 5 * u + 5]).reshape(len(unit), 4, 4, -1)
        for m, (d, dy) in enumerate(unit):
            out[pl.ds(4 * lax.rem(place[0] + dy, 4), 4), 4 * d : 4 * d + 4, :] = value[m]


def collect(place, shards, sums):
    args = [term for terms in sums for term in terms]
    return call(functools.partial(collect_kernel, shards), args, [((16, 16, 1024), F32)], place=place, limit=16)[0]


def join_kernel(*refs):
    out = refs[-1]
    out[:, :, :512] = total(*refs[:5]).reshape(16, 16, -1)
    out[:, :, 512:] = total(*refs[5:-1]).reshape(16, 16, -1)


def join(one, other):
    return call(join_kernel, [*one, *other], [((16, 16, 1024), F32)])[0]


def place_kernel(column, n_parts, place, *refs):
    parts, (out, block, done) = refs[:n_parts], refs[-3:]
    pieces = [(part, at) for part in parts for at in range(0, part.shape[2], 512)]
    copies = []
    for s in range(16):
        for q, (part, at) in enumerate(pieces):
            for d in range(4):
                block[q, s, :, (s // 4 + d) % 4, :] = part[s, 4 * d : 4 * d + 4, at : at + 512]
            columns = pl.ds(pl.multiple_of(512 * column(place, s, q), 512), 512)
            copies.append(pltpu.make_async_copy(block.at[q, s], out.at[:, :, columns], done.at[16 * q + s]))
            copies[-1].start()
    for copy in copies:
        copy.wait()


def placed(place, parts, column, out=None):
    n = sum(part.shape[2] // 512 for part in parts)
    return call(
        functools.partial(place_kernel, column, len(parts)),
        parts if out is None else [*parts, out],
        [((4, 4, 32768), F32)],
        [pltpu.VMEM((n, 16, 4, 4, 512), F32), pltpu.SemaphoreType.DMA((16 * n,))],
        place,
        in_hbm=(len(parts),),
        out_hbm=(0,),
        aliases=None if out is None else {1 + len(parts): 0},
    )[0]


def own_column(place, s, q):
    return s * 4 + place[1] * 2 + lax.rem(place[2] + q, 2)


def next_column(place, s, q):
    core = lax.rem(place[2] + q, 2)
    z = lax.rem(2 * (s // 4) + place[1] + 9 - 2 * core, 8)
    return ((z // 2) * 4 + s % 4) * 4 + lax.rem(z, 2) * 2 + core


def local(integrals, amplitudes):
    place = jnp.stack([lax.axis_index(n).astype(jnp.int32) for n in ("y", "zl", "c", "x")])
    kc = integrals.shape[1]
    (t0,) = call(turn_kernel, [jnp.transpose(amplitudes, (1, 2, 0))], [((4, 16, kc), F32)], place=place)

    t1, t3 = move(t0, z=-2), move(t0, z=2)
    low0, high0, far0 = move(t0, y=1), move(t0, y=-1), move(t0, y=2)
    w = halved(integrals)

    t1, t3, low0, high0, far0 = after((t1, t3, low0, high0, far0))
    to_near, to_far = call(last_kernel, [t1, t3], [((4, 8, kc), F32)] * 2)
    t2 = whole_of(move(to_near, z=-2), move(to_far, z=2))
    t13 = pair(t1, t3)
    low13, high13 = move(t13, y=1), move(t13, y=-1)
    t2, low13, high13 = after((t2, low13, high13))
    w1 = halved(move(after(integrals, t2), c=1))
    low2, high2 = forward(t2, low13, high13)
    w2 = move(after(integrals, t2), apart=1)

    def whole(n, lead=None):
        return ((n, lead, 0), (n, lead, 8))

    def halves(at):
        return ((0, None, at), (1, None, at))

    shards = [
        [(0, 0), (0, 1), (0, 2), (0, 3), (1, 0), (1, 1), (1, 3), (3, 0), (3, 1), (3, 3)],
        [(1, 2), (3, 2), (2, 0), (2, 1), (2, 2), (2, 3)],
    ]
    sources = [whole(0), whole(1), whole(2), whole(3)] + [whole(n, g) for g in range(2) for n in (4, 5, 6)]
    parts0, unit0 = first(place, sources, [t0, high0, far0, low0, t13, high13, low13], w, w1)
    come0 = ring_first(parts0)

    low2, high2 = after((low2, high2), parts0)
    far2 = last(low2, high2)
    sources = [halves(16), halves(24), whole(4), whole(1), ((2, None, 0), (3, None, 0)), whole(0)]
    parts1, unit1 = first(place, sources, [low2, high2, *far2, t2], w, w1)
    come1 = ring_first(parts1)

    units = [*unit0, *unit1]
    added0 = ring_add(parts0, come0)
    sum0 = ring_second(parts0, come0, added0)
    added1 = ring_add(after(parts1, come0), come1)
    sum1 = ring_second(parts1, come1, added1)
    parts2 = second_ring(place, shards, units, after(w2, added1, added0))
    w3 = move(after(w2, parts1, come0, added0), c=1)
    come2 = ring_first(parts2)
    parts3 = second_ring(place, shards, units, after(w3, parts2, sum0))
    come3 = ring_first(parts3)
    sum2 = ring_second(parts2, come2, ring_add(parts2, come2))
    sum3 = ring_second(parts3, come3, ring_add(parts3, come3))

    def relaid(value):
        return lax.all_to_all(value, ("zh", "y"), split_axis=0, concat_axis=0, tiled=True)

    out = placed(place, [relaid(collect(place, shards, after([sum0, sum1], parts3, come2)))], own_column)
    return placed(place, [relaid(join(sum2, sum3))], next_column, out)


def solution(mesh):
    fine = Mesh(mesh.devices.reshape(SIZES), AXES)
    return jax.shard_map(
        local,
        mesh=fine,
        in_specs=(P(("zh", "y", "zl", "c"), "x"), P("x", ("zl", "c"), ("zh", "y"))),
        out_specs=P(("zl", "c", "x"), ("zh", "y"), None),
        check_vma=False,
    )
```

```python
import functools

import jax
import jax.numpy as jnp
import numpy as np
from jax import lax
from jax.experimental import pallas as pl
from jax.experimental.pallas import tpu as pltpu
from jax.sharding import Mesh
from jax.sharding import PartitionSpec as P

AXES = ("zh", "y", "zl", "c", "x")
SIZES = (4, 4, 2, 2, 4)
VMEM = pl.BlockSpec(memory_space=pltpu.VMEM)
SMEM = pl.BlockSpec(memory_space=pltpu.SMEM)
HBM = pl.BlockSpec(memory_space=pltpu.MemorySpace.HBM)
F32, BF16 = jnp.float32, jnp.bfloat16


def move(value, x=0, y=0, z=0, c=0, apart=0):
    pairs = []
    for source, (at_zh, at_y, at_zl, at_c, at_x) in enumerate(np.ndindex(*SIZES)):
        to_z = (2 * at_zh + at_zl + z + (2 * at_c - 1) * apart) % 8
        to = (to_z // 2, (at_y + y) % 4, to_z % 2, (at_c + c) % 2, (at_x + x) % 4)
        pairs.append((source, int(np.ravel_multi_index(to, SIZES))))
    return lax.ppermute(value, AXES, pairs)


def after(value, *others):
    return lax.optimization_barrier((value, others))[0]


def call(kernel, args, shapes, scratch=(), place=None, in_hbm=(), out_hbm=(), aliases=None, limit=12):
    count = len(args)
    specs = [HBM if n in in_hbm else VMEM for n in range(count)]
    if place is not None:
        args, specs = [place, *args], [SMEM, *specs]
    return pl.pallas_call(
        kernel,
        in_specs=specs,
        out_specs=[HBM if n in out_hbm else VMEM for n in range(len(shapes))],
        out_shape=[jax.ShapeDtypeStruct(*shape) for shape in shapes],
        scratch_shapes=list(scratch),
        input_output_aliases=aliases or {},
        compiler_params=pltpu.CompilerParams(vmem_limit_bytes=limit * 2**20),
        cost_estimate=pl.CostEstimate(flops=0, bytes_accessed=0, transcendentals=0),
    )(*args)


def split(value):
    high = value.astype(BF16)
    return high, (value - high.astype(F32)).astype(BF16)


def turn_kernel(place, value, out):
    for j in range(4):
        out[j] = value[:, j, :]


def halved_kernel(value, high, low):
    high[...], low[...] = split(value[...])


def halved(value):
    return call(halved_kernel, [value], [(value.shape, BF16)] * 2)


def pair_kernel(one, other, out):
    out[0] = one[...]
    out[1] = other[...]


def pair(one, other):
    return call(pair_kernel, [one, other], [((2, *one.shape), F32)])[0]


def forward_kernel(own, low, high, to_right, to_left):
    for out, come, start in ((to_right, low, 0), (to_left, high, 8)):
        out[:, :16] = own[...]
        out[:, 16:24] = come[0, :, start : start + 8]
        out[:, 24:] = come[1, :, start : start + 8]


def forward(own, low, high):
    shape = (4, 32, own.shape[2])
    to_right, to_left = call(forward_kernel, [own, low, high], [(shape, F32)] * 2)
    return move(to_right, y=1), move(to_left, y=-1)


def last_kernel(low, high, to_right, to_left):
    to_right[...] = low[:, :8]
    to_left[...] = high[:, 8:16]


def last(low, high):
    shape = (4, 8, low.shape[2])
    to_right, to_left = call(last_kernel, [low, high], [(shape, F32)] * 2)
    return move(to_right, y=1), move(to_left, y=-1)


def whole_kernel(low, high, out):
    out[:, :8] = low[...]
    out[:, 8:] = high[...]


def whole_of(low, high):
    return call(whole_kernel, [low, high], [((4, 16, low.shape[2]), F32)])[0]


def product(t_high, t_low, w_high, w_low):
    dot = functools.partial(lax.dot_general, dimension_numbers=(((1,), (1,)), ((), ())), preferred_element_type=F32)
    return dot(t_high, w_high) + (dot(t_high, w_low) + dot(t_low, w_high))


def store(blocks, at, outs):
    half = blocks.shape[1] // 2
    columns = slice(at, at + blocks.shape[2])
    to_right, to_left, right_low, left_high, own = outs
    to_right[:half, columns] = blocks[2, :half]
    to_right[half:, columns] = blocks[1, half:]
    to_left[:half, columns] = blocks[2, half:]
    to_left[half:, columns] = blocks[3, :half]
    right_low[:, columns] = blocks[1, :half]
    left_high[:, columns] = blocks[3, half:]
    own[:, columns] = blocks[0]


def shapes_of(rows, columns):
    return [((n, columns), F32) for n in (rows, rows, rows // 2, rows // 2, rows)]


def first_kernel(sources, n_parts, place, *refs):
    n = len(sources)
    parts, ws, outs = refs[:n_parts], refs[n_parts : n_parts + 4], refs[n_parts + 4 : n_parts + 9]
    t_high, t_low, t = refs[-3:]
    for m, halves in enumerate(sources):
        for x in range(4):
            number, lead, start = halves[x // 2]
            part = parts[number] if lead is None else parts[number].at[lead]
            start = start + 4 * (x % 2)
            e = lax.rem(x - place[3] + 4, 4)
            for j in range(4):
                t[e, m, 4 * j : 4 * j + 4, :] = part[j, start : start + 4, :]
    t_high[...], t_low[...] = split(t[...].reshape(64 * n, -1))
    for k in range(4):
        rows = slice(256 * (k % 2), 256 * (k % 2) + 256)
        block = product(t_high[...], t_low[...], ws[k // 2 * 2][rows, :], ws[k // 2 * 2 + 1][rows, :])
        store(block.reshape(4, 16 * n, 256), 256 * k, outs)


def first(place, sources, parts, w0, w1):
    kc, n = w0[0].shape[1], len(sources)
    out = call(
        functools.partial(first_kernel, sources, len(parts)),
        [*parts, *w0, *w1],
        shapes_of(16 * n, 1024) + [((64 * n, kc), BF16)] * 2,
        [pltpu.VMEM((4, n, 16, kc), F32)],
        place,
        limit=16,
    )
    return out[:5], out[5:]


def second_rows(shards, place, units, w_high, w_low, buffer):
    for u, unit in enumerate(shards):
        block = product(units[2 * u][...], units[2 * u + 1][...], w_high, w_low)
        block = block.reshape(4, len(unit), 4, 4, 256)
        for m, (d, dy) in enumerate(unit):
            r = 4 * lax.rem(place[0] + dy, 4)
            buffer[:, pl.ds(r, 4), 4 * d : 4 * d + 4, :] = block[:, m]


def second_ring_kernel(shards, place, *refs):
    units, w, outs, buffer = refs[:4], refs[4], refs[5:10], refs[10]
    for n in range(2):
        second_rows(shards, place, units, *split(w[256 * n : 256 * n + 256, :]), buffer)
        store(buffer[...].reshape(4, 256, 256), 256 * n, outs)


def second_ring(place, shards, units, w):
    kernel = functools.partial(second_ring_kernel, shards)
    return call(kernel, [*units, w], shapes_of(256, 512), [pltpu.VMEM((4, 16, 16, 256), F32)], place)


def add_kernel(right_low, left_high, from_left, from_right, to_right, to_left):
    half = right_low.shape[0]
    to_right[...] = right_low[...] + from_left[:half]
    to_left[...] = left_high[...] + from_right[:half]


def ring_first(parts):
    return move(parts[0], x=1), move(parts[1], x=-1)


def ring_add(parts, come):
    return call(add_kernel, [*parts[2:4], *come], [(parts[2].shape, F32)] * 2)


def ring_second(parts, come, added):
    return [parts[4], *come, move(added[0], x=1), move(added[1], x=-1)]


def total(own, from_left, from_right, from_left2, from_right2):
    half = own.shape[0] // 2
    low = own[:half] + from_right[half:] + from_left2[...]
    high = own[half:] + from_left[half:] + from_right2[...]
    return jnp.concatenate([low, high])


def collect_kernel(shards, place, *refs):
    out = refs[-1]
    for u, unit in enumerate(shards):
        value = total(*refs[5 * u : 5 * u + 5]).reshape(len(unit), 4, 4, -1)
        for m, (d, dy) in enumerate(unit):
            out[pl.ds(4 * lax.rem(place[0] + dy, 4), 4), 4 * d : 4 * d + 4, :] = value[m]


def collect(place, shards, sums):
    args = [term for terms in sums for term in terms]
    return call(functools.partial(collect_kernel, shards), args, [((16, 16, 1024), F32)], place=place, limit=16)[0]


def join_kernel(*refs):
    out = refs[-1]
    out[:, :, :512] = total(*refs[:5]).reshape(16, 16, -1)
    out[:, :, 512:] = total(*refs[5:-1]).reshape(16, 16, -1)


def join(one, other):
    return call(join_kernel, [*one, *other], [((16, 16, 1024), F32)])[0]


def place_kernel(column, n_parts, place, *refs):
    parts, (out, block, done) = refs[:n_parts], refs[-3:]
    pieces = [(part, at) for part in parts for at in range(0, part.shape[2], 512)]
    copies = []
    for s in range(16):
        for q, (part, at) in enumerate(pieces):
            for d in range(4):
                block[q, s, :, (s // 4 + d) % 4, :] = part[s, 4 * d : 4 * d + 4, at : at + 512]
            columns = pl.ds(pl.multiple_of(512 * column(place, s, q), 512), 512)
            copies.append(pltpu.make_async_copy(block.at[q, s], out.at[:, :, columns], done.at[16 * q + s]))
            copies[-1].start()
    for copy in copies:
        copy.wait()


def placed(place, parts, column, out=None):
    n = sum(part.shape[2] // 512 for part in parts)
    return call(
        functools.partial(place_kernel, column, len(parts)),
        parts if out is None else [*parts, out],
        [((4, 4, 32768), F32)],
        [pltpu.VMEM((n, 16, 4, 4, 512), F32), pltpu.SemaphoreType.DMA((16 * n,))],
        place,
        in_hbm=(len(parts),),
        out_hbm=(0,),
        aliases=None if out is None else {1 + len(parts): 0},
    )[0]


def own_column(place, s, q):
    return s * 4 + place[1] * 2 + lax.rem(place[2] + q, 2)


def next_column(place, s, q):
    core = lax.rem(place[2] + q, 2)
    z = lax.rem(2 * (s // 4) + place[1] + 9 - 2 * core, 8)
    return ((z // 2) * 4 + s % 4) * 4 + lax.rem(z, 2) * 2 + core


def local(integrals, amplitudes):
    place = jnp.stack([lax.axis_index(n).astype(jnp.int32) for n in ("y", "zl", "c", "x")])
    kc = integrals.shape[1]
    (t0,) = call(turn_kernel, [jnp.transpose(amplitudes, (1, 2, 0))], [((4, 16, kc), F32)], place=place)

    t1, t3 = move(t0, z=-2), move(t0, z=2)
    low0, high0, far0 = move(t0, y=1), move(t0, y=-1), move(t0, y=2)
    w = halved(integrals)

    t1, t3, low0, high0, far0 = after((t1, t3, low0, high0, far0))
    to_near, to_far = call(last_kernel, [t1, t3], [((4, 8, kc), F32)] * 2)
    t2 = whole_of(move(to_near, z=-2), move(to_far, z=2))
    t13 = pair(t1, t3)
    low13, high13 = move(t13, y=1), move(t13, y=-1)
    t2, low13, high13 = after((t2, low13, high13))
    w1 = halved(move(after(integrals, t2), c=1))
    low2, high2 = forward(t2, low13, high13)
    w2 = move(after(integrals, t2), apart=1)

    def whole(n, lead=None):
        return ((n, lead, 0), (n, lead, 8))

    def halves(at):
        return ((0, None, at), (1, None, at))

    shards = [
        [(0, 0), (0, 1), (0, 2), (0, 3), (1, 0), (1, 1), (1, 3), (3, 0), (3, 1), (3, 3)],
        [(1, 2), (3, 2), (2, 0), (2, 1), (2, 2), (2, 3)],
    ]
    sources = [whole(0), whole(1), whole(2), whole(3)] + [whole(n, g) for g in range(2) for n in (4, 5, 6)]
    parts0, unit0 = first(place, sources, [t0, high0, far0, low0, t13, high13, low13], w, w1)
    come0 = ring_first(parts0)

    low2, high2 = after((low2, high2), parts0)
    far2 = last(low2, high2)
    sources = [halves(16), halves(24), whole(4), whole(1), ((2, None, 0), (3, None, 0)), whole(0)]
    parts1, unit1 = first(place, sources, [low2, high2, *far2, t2], w, w1)
    come1 = ring_first(parts1)

    units = [*unit0, *unit1]
    added0 = ring_add(parts0, come0)
    sum0 = ring_second(parts0, come0, added0)
    added1 = ring_add(after(parts1, come0), come1)
    sum1 = ring_second(parts1, come1, added1)
    parts2 = second_ring(place, shards, units, after(w2, added1, added0))
    w3 = move(after(w2, parts1, come0, added0), c=1)
    come2 = ring_first(parts2)
    parts3 = second_ring(place, shards, units, after(w3, parts2, sum0))
    come3 = ring_first(parts3)
    sum2 = ring_second(parts2, come2, ring_add(parts2, come2))
    sum3 = ring_second(parts3, come3, ring_add(parts3, come3))

    def relaid(value):
        return lax.all_to_all(value, ("zh", "y"), split_axis=0, concat_axis=0, tiled=True)

    out = placed(place, [relaid(collect(place, shards, after([sum0, sum1], parts3, come2)))], own_column)
    rest, out = after((join(sum2, sum3), out))
    return placed(place, [relaid(rest)], next_column, out)


def solution(mesh):
    fine = Mesh(mesh.devices.reshape(SIZES), AXES)
    return jax.shard_map(
        local,
        mesh=fine,
        in_specs=(P(("zh", "y", "zl", "c"), "x"), P("x", ("zl", "c"), ("zh", "y"))),
        out_specs=P(("zl", "c", "x"), ("zh", "y"), None),
        check_vma=False,
    )
```
